128 devices in a mesh: blk: 64 (over y, z_hi, x, core), grp: 2 (over z_lo).
Axes of the slice: x: 4, y: 4, z: 4 (z_hi: 2, z_lo: 2; z = z_hi * 2 + z_lo), core: 2. Of those that a mesh axis runs over, the one named last changes fastest.
Arguments:
- orbitals: float32 [64, 128, 128, 128], P(None, 'blk', 'grp'), may hold values from -6 to 6
- occupations: float32 [64], replicated, may hold values from 0.5 to 2
- band_block: int32 [64], replicated, may hold values from 0 to 63, as said below
- cycle: int32 [64], replicated, may hold values from 0 to 63, each once
Outputs:
- exchange_field: float32 [64, 128, 128, 128], P(None, 'blk', 'grp')
The draws below stay inside these ranges and needn't reach their ends.
Inputs may be any that keep to these rules, and one draw needn't show every extreme that they name: `band_block`: each of the 64 blocks is named by exactly one band. Each block stands at exactly one cycle position.
All inputs are finite; a program needn't handle non-finite values.
Results may differ from the reference program's by a relative error of at most 0.0003.
Values sent between devices are 32-bit elements; how exact they have to be, the bound alone decides.
A program may use at most 128 MiB of HBM per device.

```python
import math
import jax
import jax.numpy as jnp
from jax import lax

BAND_DEV = 1
NX = 128
NY = 128
NZ = 128
NBLK = 64
NBANDS = 64


def draw_orbitals(key, part):
    key = jax.random.fold_in(key, 5)
    values = jax.random.normal(key, (NBANDS, NX, NY, NZ), jnp.float32)
    return jnp.clip(values, -6.0, 6.0)


def draw_band_block(key, part):
    key = jax.random.fold_in(key, 11)
    labels = jnp.arange(NBANDS, dtype=jnp.int32) // BAND_DEV
    return jax.random.permutation(key, labels)


def setup_inputs(seed: int = 0) -> dict:
    key_list = jax.random.split(jax.random.key(seed), 5)
    orbitals = draw_orbitals(jax.random.fold_in(key_list[4], 71), 0)
    occupations = jnp.clip(jax.random.uniform(key_list[1], (NBANDS,), jnp.float32, 0.5, 2.0), 0.5, 2.0)
    band_block = draw_band_block(jax.random.fold_in(key_list[4], 71), 0)
    cycle = jax.random.permutation(key_list[3], NBLK).astype(jnp.int32)
    return dict(orbitals=orbitals, occupations=occupations, band_block=band_block, cycle=cycle)


screening = 0.05


def kernel_table(size_x, size_y, size_z):
    def squared(length):
        index = jnp.arange(length, dtype=jnp.int32)
        folded = jnp.where(index <= length // 2, index, index - length).astype(jnp.float32)
        return (2.0 * math.pi / length * folded) ** 2
    total = squared(size_x)[:, None, None] + squared(size_y)[None, :, None] + squared(size_z)[None, None, :]
    safe_total = jnp.where(total > 0, total, 1.0)
    screened = (1.0 - jnp.exp(-safe_total / (4.0 * screening ** 2))) / safe_total
    return jnp.where(total > 0, screened, 1.0 / (4.0 * screening ** 2))


def convolve(density, kernel):
    spectrum = jnp.fft.fftn(density, axes=(1, 2, 3))
    return jnp.real(jnp.fft.ifftn(spectrum * kernel, axes=(1, 2, 3))).astype(jnp.float32)


def reference(orbitals, occupations, band_block, cycle):
    kernel = kernel_table(NX, NY, NZ)
    order = jnp.argsort(band_block, stable=True).astype(jnp.int32)
    cycle_rows = order.reshape(NBLK, BAND_DEV)[cycle].reshape(-1)
    blocks_all = orbitals[cycle_rows].reshape(NBLK, BAND_DEV, NX, NY, NZ)
    weights = occupations[cycle_rows].reshape(NBLK, BAND_DEV)

    def visit(result, position):
        first = blocks_all[position]
        first_weight = weights[position]
        for offset in (1, 2):
            other_pos = (position - offset) % NBLK
            second = blocks_all[other_pos]
            second_weight = weights[other_pos]
            density = (first[:, None] * second[None, :]).reshape(BAND_DEV * BAND_DEV, NX, NY, NZ)
            field = convolve(density, kernel).reshape(BAND_DEV, BAND_DEV, NX, NY, NZ)
            to_first = jnp.sum(field * (second_weight[:, None, None, None] * second)[None], axis=1)
            to_second = jnp.sum(field * (first_weight[:, None, None, None] * first)[:, None], axis=0)
            result = result.at[position].add(to_first)
            result = result.at[other_pos].add(to_second)
        return result, None

    start = jnp.zeros((NBLK, BAND_DEV, NX, NY, NZ), jnp.float32)
    result, unused = lax.scan(visit, start, jnp.arange(NBLK, dtype=jnp.int32))
    flat = result.reshape(NBANDS, NX, NY, NZ)
    return jnp.zeros((NBANDS, NX, NY, NZ), jnp.float32).at[cycle_rows].set(flat)
```

```python
import functools
import math

import jax
import jax.numpy as jnp
import ml_dtypes
import numpy as np
from jax import lax
from jax.experimental import pallas as pl
from jax.experimental.pallas import tpu as pltpu
from jax.sharding import PartitionSpec as P

screening = 0.05
MESH = pl.DeviceIdType.MESH
MIB = 2**20


def hartley_split(length):
    index = np.arange(length)
    angle = 2.0 * math.pi / length * (index[:, None] * index[None, :] % length)
    exact = (np.cos(angle) + np.sin(angle)).astype(np.float64)
    high = exact.astype(ml_dtypes.bfloat16)
    low = (exact - high.astype(np.float64)).astype(ml_dtypes.bfloat16)
    return np.block([[high, low], [high, np.zeros_like(high)]])


def split(value, axis):
    high = value.astype(jnp.bfloat16)
    low = (value - high.astype(jnp.float32)).astype(jnp.bfloat16)
    return jnp.concatenate([high, low], axis=axis)


def times_right(value, table):
    length = table.shape[0] // 2
    both = jnp.dot(split(value, 1), table, preferred_element_type=jnp.float32)
    return both[:, :length] + both[:, length:]


def times_left(table, value):
    length = table.shape[0] // 2
    both = jnp.dot(table, split(value, 0), preferred_element_type=jnp.float32)
    return both[:length] + both[length:]


def squared(index, length):
    folded = jnp.where(index <= length // 2, index, index - length).astype(jnp.float32)
    return (2.0 * math.pi / length * folded) ** 2


def exchange_kernel(
    sizes,
    rows_ref,
    weight_ref,
    phi_ref,
    right_z_ref,
    left_y_ref,
    left_x_ref,
    field_ref,
    outgoing,
    grid,
    turned,
    kernel_table,
    arrived,
    out_sem,
    in_sem,
    back_out_sem,
    back_in_sem,
):
    blocks, size_x, size_y, size_z, local_x = sizes
    half_y = size_y // 2
    plane_rows = local_x * half_y
    blk = lax.axis_index("blk")
    grp = lax.axis_index("grp")
    other = 1 - grp
    me = blk * 2 + grp

    def hop(step):
        return (step * (step + 1) // 2) % blocks

    barrier = pltpu.get_barrier_semaphore()
    pl.semaphore_signal(barrier, inc=1, device_id=(blk, other), device_id_type=MESH)

    @pl.loop(1, blocks)
    def _(step):
        target = (blk + hop(step)) % blocks
        for side in range(2):
            pl.semaphore_signal(barrier, inc=1, device_id=(target, side), device_id_type=MESH)

    pl.semaphore_wait(barrier, 2 * blocks - 1)

    def density(position, offset):
        first = phi_ref[rows_ref[position]]
        second = phi_ref[rows_ref[(position + blocks - offset) % blocks]]
        return times_right(first * second, right_z_ref[...])

    def here(ref):
        return ref.at[pl.ds(blk * local_x, local_x), pl.ds(grp * half_y, half_y)]

    def send(target, side, slot):
        outgoing[slot] = density(target, side + 1).reshape(local_x, half_y, size_z)
        pltpu.make_async_remote_copy(
            src_ref=outgoing.at[slot],
            dst_ref=here(grid),
            send_sem=out_sem,
            recv_sem=in_sem.at[blk],
            device_id=(target, side),
            device_id_type=MESH,
        ).start()

    send(blk, other, 1)

    @pl.loop(1, blocks)
    def _(step):
        target = (blk + hop(step)) % blocks
        for side in range(2):
            send(target, side, 2 * step + side)

    own = density(blk, grp + 1).reshape(local_x, half_y, size_z)
    grid[pl.ds(blk * local_x, local_x), pl.ds(grp * half_y, half_y)] = own
    field_ref[...] = jnp.zeros_like(field_ref)

    across = squared(lax.broadcasted_iota(jnp.int32, (size_x, size_z), 0), size_x) + squared(
        lax.broadcasted_iota(jnp.int32, (size_x, size_z), 1), size_z
    )

    @pl.loop(0, size_y // 2 + 1)
    def _(index):
        total = across + squared(jnp.full((size_x, size_z), index, jnp.int32), size_y)
        safe_total = jnp.where(total > 0, total, 1.0)
        screened = (1.0 - jnp.exp(-safe_total / (4.0 * screening**2))) / safe_total
        value = jnp.where(total > 0, screened, 1.0 / (4.0 * screening**2))
        kernel_table[index] = value * (1.0 / (size_x * size_y * size_z))

    def turn_planes(source):
        planes = [grid[source * local_x + j] for j in range(local_x)]
        result = times_left(left_y_ref[...], jnp.concatenate(planes, axis=1))
        for j in range(local_x):
            turned[pl.ds(source * local_x + j, size_y, stride=size_x), :] = result[
                :, j * size_z : (j + 1) * size_z
            ]

    half_plane = here(grid)
    pltpu.make_async_copy(half_plane, half_plane, in_sem.at[blk]).wait()
    turn_planes(blk)

    @pl.loop(1, blocks)
    def _(step):
        source = (blk + blocks - hop(step)) % blocks
        landed = grid.at[pl.ds(source * local_x, local_x)]
        pltpu.make_async_copy(landed, landed, in_sem.at[source]).wait()
        turn_planes(source)

    group = 8

    @pl.loop(0, size_y // group)
    def _(part):
        lines = [part * group + j for j in range(group)]
        value = jnp.concatenate([turned[pl.ds(k * size_x, size_x), :] for k in lines], axis=1)
        value = times_left(left_x_ref[...], value)
        factor = [kernel_table[jnp.minimum(k, size_y - k)] for k in lines]
        value = times_left(left_x_ref[...], value * jnp.concatenate(factor, axis=1))
        for j, k in enumerate(lines):
            turned[pl.ds(k * size_x, size_x), :] = value[:, j * size_z : (j + 1) * size_z]

    def turn_back(target):
        lines = [
            turned[pl.ds(target * local_x + j, size_y, stride=size_x), :] for j in range(local_x)
        ]
        result = times_left(left_y_ref[...], jnp.concatenate(lines, axis=1))
        for j in range(local_x):
            grid[target * local_x + j] = result[:, j * size_z : (j + 1) * size_z]

    def send_back(target, side):
        pltpu.make_async_remote_copy(
            src_ref=grid.at[pl.ds(target * local_x, local_x), pl.ds(side * half_y, half_y)],
            dst_ref=arrived.at[me],
            send_sem=back_out_sem,
            recv_sem=back_in_sem.at[blk],
            device_id=(target, side),
            device_id_type=MESH,
        ).start()

    turn_back(blk)
    send_back(blk, other)

    @pl.loop(1, blocks)
    def _(step):
        target = (blk + hop(step)) % blocks
        turn_back(target)
        for side in range(2):
            send_back(target, side)

    arrived[me] = grid[pl.ds(blk * local_x, local_x), pl.ds(grp * half_y, half_y)]

    def collect(position):
        def weighted(at):
            return weight_ref[at] * phi_ref[rows_ref[at]]

        own = weighted(position)
        total = jnp.zeros((plane_rows, size_z), jnp.float32)
        for offset in (1, 2):
            behind = (position + blocks - offset) % blocks
            value = arrived[position * 2 + offset - 1].reshape(plane_rows, size_z)
            value = times_right(value, right_z_ref[...])
            total = total + value * weighted(behind)
            field_ref[behind] += value * own
        field_ref[position] += total

    pltpu.make_async_copy(arrived.at[me], arrived.at[me], back_in_sem.at[blk]).wait()
    collect(blk)

    @pl.loop(1, blocks)
    def _(step):
        source = (blk + blocks - hop(step)) % blocks
        landed = arrived.at[pl.ds(source * 2, 2)]
        pltpu.make_async_copy(landed, landed, back_in_sem.at[source]).wait()
        collect(source)

    sent = outgoing.at[pl.ds(1, 2 * blocks - 1)]
    pltpu.make_async_copy(sent, sent, out_sem).wait()
    pltpu.make_async_copy(sent, sent, back_out_sem).wait()


def place_kernel(nbands, rows_ref, field_ref, out_ref, sem):
    copies = [
        pltpu.make_async_copy(field_ref.at[p], out_ref.at[rows_ref[p]], sem.at[p])
        for p in range(nbands)
    ]
    for copy in copies:
        copy.start()
    for copy in copies:
        copy.wait()


def local(orbitals, occupations, band_block, cycle):
    blocks = lax.axis_size("blk")
    nbands, local_x, half_y, size_z = orbitals.shape
    size_x = local_x * blocks
    size_y = half_y * 2
    plane_rows = local_x * half_y
    f32 = jnp.float32

    here = cycle[:, None] == band_block[None, :]
    rows = jnp.sum(jnp.where(here, jnp.arange(nbands, dtype=jnp.int32)[None], 0), axis=1)
    weights = jnp.sum(jnp.where(here, occupations[None], 0.0), axis=1)

    vmem = pl.BlockSpec(memory_space=pltpu.VMEM)
    smem = pl.BlockSpec(memory_space=pltpu.SMEM)
    field = pl.pallas_call(
        functools.partial(exchange_kernel, (blocks, size_x, size_y, size_z, local_x)),
        out_shape=jax.ShapeDtypeStruct((nbands, plane_rows, size_z), f32),
        in_specs=[smem, smem, vmem, vmem, vmem, vmem],
        out_specs=vmem,
        scratch_shapes=[
            pltpu.VMEM((2 * blocks, local_x, half_y, size_z), f32),
            pltpu.VMEM((size_x, size_y, size_z), f32),
            pltpu.VMEM((size_y * size_x, size_z), f32),
            pltpu.VMEM((size_y // 2 + 1, size_x, size_z), f32),
            pltpu.VMEM((2 * blocks, local_x, half_y, size_z), f32),
            pltpu.SemaphoreType.DMA,
            pltpu.SemaphoreType.DMA((blocks,)),
            pltpu.SemaphoreType.DMA,
            pltpu.SemaphoreType.DMA((blocks,)),
        ],
        compiler_params=pltpu.CompilerParams(
            collective_id=0, has_side_effects=True, vmem_limit_bytes=60 * MIB
        ),
    )(
        rows,
        weights,
        orbitals.reshape(nbands, plane_rows, size_z),
        jnp.asarray(hartley_split(size_z)),
        jnp.asarray(hartley_split(size_y).T),
        jnp.asarray(hartley_split(size_x).T),
    )
    placed = pl.pallas_call(
        functools.partial(place_kernel, nbands),
        out_shape=jax.ShapeDtypeStruct((nbands, plane_rows, size_z), f32),
        in_specs=[smem, pl.BlockSpec(memory_space=pl.ANY)],
        out_specs=pl.BlockSpec(memory_space=pl.ANY),
        scratch_shapes=[pltpu.SemaphoreType.DMA((nbands,))],
    )(rows, field)
    return placed.reshape(orbitals.shape)


def solution(mesh):
    return jax.shard_map(
        local,
        mesh=mesh,
        in_specs=(P(None, "blk", "grp", None), P(), P(), P()),
        out_specs=P(None, "blk", "grp", None),
        check_vma=False,
    )
```

```python
import functools
import itertools
import math
import random

import jax
import jax.numpy as jnp
import ml_dtypes
import numpy as np
from jax import lax
from jax.experimental import pallas as pl
from jax.experimental.pallas import tpu as pltpu
from jax.sharding import PartitionSpec as P

screening = 0.05
MESH = pl.DeviceIdType.MESH
MIB = 2**20
f32 = jnp.float32


def hartley(length):
    index = np.arange(length)
    angle = 2.0 * math.pi / length * (index[:, None] * index[None, :] % length)
    return np.cos(angle) + np.sin(angle)


def pieces(table, axis):
    high = table.astype(ml_dtypes.bfloat16)
    low = (table - high.astype(np.float64)).astype(ml_dtypes.bfloat16)
    return jnp.asarray(np.concatenate([high, high, low], axis=axis))


def split(value, axis):
    high = value.astype(jnp.bfloat16)
    low = (value - high.astype(f32)).astype(jnp.bfloat16)
    return jnp.concatenate([high, low, high], axis=axis)


def times_right(value, table):
    return jnp.dot(split(value, 1), table, preferred_element_type=f32)


def times_left(table, value):
    return jnp.dot(table, split(value, 0), preferred_element_type=f32)


def planes_table(size_z):
    half = size_z // 2
    table = hartley(size_z)
    full = np.zeros((2, size_z, 2, 2, half))
    for plane in range(2):
        for part in range(2):
            full[plane, :, part, plane, :] = table[:, part * half : (part + 1) * half]
    return full.reshape(2 * size_z, 2 * size_z)


def torus_of(blocks):
    return (4, 4, 4) if blocks == 64 else (blocks // 2, 1, 2)


def message_order(blocks):
    torus = torus_of(blocks)
    everywhere = itertools.product(*(range(size) for size in torus))
    triples, seen = [], {(0, 0, 0)}
    for offset in everywhere:
        if offset not in seen:
            turns = [offset]
            if torus[0] == torus[1] == torus[2]:
                turns = list(dict.fromkeys(offset[k:] + offset[:k] for k in range(3)))
            seen.update(turns)
            triples.append(turns)
    random.Random(1).shuffle(triples)
    triples.sort(key=lambda turns: sum(min(d, n - d) for d, n in zip(turns[0], torus)))
    mixed = []
    while triples:
        mixed.append(triples.pop(0))
        if triples:
            mixed.append(triples.pop())
    order = [(0, 0, 0, 1)]
    order += [d + (core,) for turns in mixed for core in (0, 1) for d in turns]
    return order + [(0, 0, 0, 0)]


def source_order(blocks, parity):
    torus = torus_of(blocks)
    due = {}
    for time, (dx, dy, dz, core) in enumerate(message_order(blocks)):
        sign = -1 if core else 1
        offset = [sign * d % n for d, n in zip((dx, dy, dz), torus)]
        block = (offset[0], offset[1], (parity - offset[2]) % torus[2] // 2, core)
        due[block] = (time, tuple(offset) + (core,))
    own = (0, 0, parity // 2, 0)
    rest = sorted(due[block] for block in due if block != own)
    return [(0, 0, 0, 0)] + [offset for time, offset in rest]


def packed(order):
    codes = [dx + 4 * dy + 16 * dz + 64 * core for dx, dy, dz, core in order]
    return [sum(c * 128**j for j, c in enumerate(codes[i : i + 4])) for i in range(0, len(codes), 4)]


def word_at(words, index):
    word = jnp.int32(words[0])
    for k in range(1, len(words)):
        word = jnp.where(index == k, jnp.int32(words[k]), word)
    return word


def offsets_in(word):
    for j in range(4):
        code = word // 128**j % 128
        yield code % 4, code // 4 % 4, code // 16 % 4, code // 64


def squared(index, length):
    folded = jnp.where(index <= length // 2, index, index - length).astype(f32)
    return (2.0 * math.pi / length * folded) ** 2


def exchange_kernel(
    sizes,
    rows_ref,
    weight_ref,
    phi_ref,
    forward_z_ref,
    inverse_z_ref,
    left_y_ref,
    forward_x_ref,
    inverse_x_ref,
    field_ref,
    outgoing,
    grid,
    turned,
    kernel_table,
    arrived,
    out_sem,
    in_sem,
    back_out_sem,
    back_in_sem,
):
    blocks, size_x, size_y, size_z = sizes
    half_y = size_y // 2
    half_z = size_z // 2
    blk = lax.axis_index("blk")
    grp = lax.axis_index("grp")
    me = blk * 2 + grp
    own_rows = pl.ds(grp * half_y, half_y)

    span_x, span_y, span_z = torus_of(blocks)
    core = blk % 2
    at_x = blk // 2 % span_x
    at_y = blk // (span_x * span_z)
    at_z = blk // (2 * span_x) % (span_z // 2) * 2 + grp
    sign = 1 - 2 * core
    messages = packed(message_order(blocks))
    sources = [packed(source_order(blocks, parity)) for parity in range(2)]

    def device(offset, direction):
        x, y, z, other_core = offset
        x = (at_x + direction * x + span_x) % span_x
        y = (at_y + direction * y + span_y) % span_y
        z = (at_z + direction * z + span_z) % span_z
        block = (y * (span_z // 2) + z // 2) * span_x + x
        return block * 2 + (core + other_core) % 2, z % 2

    def targets(index):
        return [device(offset, sign) for offset in offsets_in(word_at(messages, index))]

    def source_blocks(index):
        pairs = [word_at(sources[parity], index) for parity in range(2)]
        word = jnp.where((core + grp) % 2 == 0, pairs[0], pairs[1])
        return [device(offset, -sign)[0] for offset in offsets_in(word)]

    count = 2 * blocks

    def every_other(act):
        @pl.loop(0, count // 4 - 1)
        def _(index):
            for j, target in enumerate(targets(index)):
                act(index * 4 + j, target)

        for j, target in enumerate(targets(count // 4 - 1)[:3]):
            act(count - 4 + j, target)

    barrier = pltpu.get_barrier_semaphore()

    def greet(slot, target):
        pl.semaphore_signal(barrier, inc=1, device_id=target, device_id_type=MESH)

    every_other(greet)
    pl.semaphore_wait(barrier, count - 1)

    def density(position, offset):
        first = phi_ref[rows_ref[position]]
        second = phi_ref[rows_ref[(position + blocks - offset) % blocks]]
        value = first * second
        return jnp.concatenate([value[:half_y], value[half_y:]], axis=1)

    def send(part, slot, target):
        pltpu.make_async_remote_copy(
            src_ref=outgoing.at[part, slot],
            dst_ref=grid.at[part, blk, own_rows],
            send_sem=out_sem,
            recv_sem=in_sem.at[part, blk],
            device_id=target,
            device_id_type=MESH,
        ).start()

    def prepare(index, sent):
        at = targets(index)
        value = jnp.concatenate([density(b, side + 1) for b, side in at], axis=0)
        value = times_right(value, forward_z_ref[...])
        for j in range(4):
            for part in range(2):
                outgoing[part, index * 4 + j] = value[
                    j * half_y : (j + 1) * half_y, part * size_z : (part + 1) * size_z
                ]
        for j in range(sent):
            send(0, index * 4 + j, at[j])

    @pl.loop(0, count // 4 - 1)
    def _(index):
        prepare(index, 4)

    prepare(count // 4 - 1, 3)
    every_other(functools.partial(send, 1))
    for part in range(2):
        grid[part, blk, own_rows] = outgoing[part, count - 1]
    field_ref[...] = jnp.zeros_like(field_ref)

    lane = lax.broadcasted_iota(jnp.int32, (size_x, size_z), 1)
    first_half = lane < half_z
    lane_half = jnp.where(first_half, 0, 1)

    def fill_table(part):
        square_x = squared(lax.broadcasted_iota(jnp.int32, (size_x, size_z), 0), size_x)
        square_z = squared(lane - half_z * lane_half + part * half_z, size_z)

        @pl.loop(0, half_y)
        def _(pair):
            total = square_x + squared(2 * pair + lane_half, size_y) + square_z
            safe_total = jnp.where(total > 0, total, 1.0)
            screened = (1.0 - jnp.exp(-safe_total / (4.0 * screening**2))) / safe_total
            value = jnp.where(total > 0, screened, 1.0 / (4.0 * screening**2))
            kernel_table[part, pair] = value * (1.0 / (size_x * size_y * size_z))

    def await_copy(ref, sem):
        pltpu.make_async_copy(ref, ref, sem).wait()

    def turn(part, index, with_own):
        at = source_blocks(index)
        for j, source in enumerate(at):
            if with_own and j == 0:
                await_copy(grid.at[part, blk, own_rows], in_sem.at[part, blk])
            else:
                await_copy(grid.at[part, source], in_sem.at[part, source])
        value = jnp.concatenate([grid[part, source] for source in at], axis=1)
        value = times_left(left_y_ref[...], value)
        for j, source in enumerate(at):
            turned[part, pl.ds(source, size_y, stride=blocks), :] = value[:, j * size_z : (j + 1) * size_z]

    def middle(part):
        group = 4
        mask = first_half[:blocks]

        @pl.loop(0, half_y // group)
        def _(index):
            pairs = [index * group + j for j in range(group)]
            lines = [2 * i + j for i in pairs for j in range(2)]
            value = [turned[part, pl.ds(k * blocks, blocks), :] for k in lines]
            both = times_left(forward_x_ref[...], jnp.concatenate(value, axis=1))
            value = []
            for j in range(group):
                a = both[:, 2 * j * size_z : (2 * j + 1) * size_z]
                b = both[:, (2 * j + 1) * size_z : (2 * j + 2) * size_z]
                stay = jnp.where(first_half, a[:size_x], b[size_x:])
                move = jnp.where(first_half, b[:size_x], a[size_x:])
                value.append((stay + pltpu.roll(move, half_z, 1)) * kernel_table[part, pairs[j]])
            both = times_left(inverse_x_ref[...], jnp.concatenate(value, axis=1))
            for j, i in enumerate(pairs):
                even = both[:blocks, j * size_z : (j + 1) * size_z]
                odd = both[blocks:, j * size_z : (j + 1) * size_z]
                moved = pltpu.roll(jnp.where(mask, odd, even), half_z, 1)
                turned[part, pl.ds(2 * i * blocks, blocks), :] = jnp.where(mask, even, moved)
                turned[part, pl.ds((2 * i + 1) * blocks, blocks), :] = jnp.where(mask, moved, odd)

    def turn_back(part, slot, target):
        block, side = target
        rows = pl.ds(pl.multiple_of(side * half_y, half_y), half_y)
        lines = turned[part, pl.ds(block, size_y, stride=blocks), :]
        grid[part, block, rows] = times_left(left_y_ref[rows, :], lines)

    def send_back(part, slot, target):
        block, side = target
        pltpu.make_async_remote_copy(
            src_ref=grid.at[part, block, pl.ds(side * half_y, half_y)],
            dst_ref=arrived.at[part, me],
            send_sem=back_out_sem,
            recv_sem=back_in_sem.at[part, blk],
            device_id=target,
            device_id_type=MESH,
        ).start()

    def give_back(part, index, sent):
        at = targets(index)
        for target in at:
            turn_back(part, None, target)
        for target in at[:sent]:
            send_back(part, None, target)

    for part in range(2):
        fill_table(part)
        turn(part, 0, True)

        @pl.loop(1, blocks // 4)
        def _(index):
            turn(part, index, False)

    for part in range(2):
        middle(part)

        @pl.loop(0, count // 4 - 1)
        def _(index):
            give_back(part, index, 4)

        give_back(part, count // 4 - 1, 3)
        arrived[part, me] = grid[part, blk, own_rows]

    def collect(index, with_own):
        at = source_blocks(index)
        for part in range(2):
            for j, source in enumerate(at):
                if with_own and j == 0:
                    await_copy(arrived.at[part, me], back_in_sem.at[part, blk])
                else:
                    landed = arrived.at[part, pl.ds(source * 2, 2)]
                    await_copy(landed, back_in_sem.at[part, source])
        slots = [source * 2 + side for source in at for side in range(2)]
        value = [jnp.concatenate([arrived[0, k], arrived[1, k]], axis=1) for k in slots]
        value = times_right(jnp.concatenate(value, axis=0), inverse_z_ref[...])
        for j, position in enumerate(at):
            own = weight_ref[position] * phi_ref[rows_ref[position]]
            total = jnp.zeros((size_y, size_z), f32)
            for side in range(2):
                behind = (position + blocks - side - 1) % blocks
                term = value[(2 * j + side) * half_y : (2 * j + side + 1) * half_y]
                term = jnp.concatenate([term[:, :size_z], term[:, size_z:]], axis=0)
                total = total + term * (weight_ref[behind] * phi_ref[rows_ref[behind]])
                field_ref[behind] += term * own
            field_ref[position] += total

    collect(0, True)

    @pl.loop(1, blocks // 4)
    def _(index):
        collect(index, False)

    for part in range(2):
        sent = outgoing.at[part, pl.ds(0, count - 1)]
        await_copy(sent, out_sem)
        await_copy(sent, back_out_sem)


def place_kernel(nbands, rows_ref, field_ref, out_ref, sem):
    copies = [
        pltpu.make_async_copy(field_ref.at[p], out_ref.at[rows_ref[p]], sem.at[p])
        for p in range(nbands)
    ]
    for copy in copies:
        copy.start()
    for copy in copies:
        copy.wait()


def local(orbitals, occupations, band_block, cycle):
    blocks = lax.axis_size("blk")
    nbands, local_x, half_y, size_z = orbitals.shape
    size_x = local_x * blocks
    size_y = half_y * 2
    plane_rows = local_x * half_y

    here = cycle[:, None] == band_block[None, :]
    rows = jnp.sum(jnp.where(here, jnp.arange(nbands, dtype=jnp.int32)[None], 0), axis=1)
    weights = jnp.sum(jnp.where(here, occupations[None], 0.0), axis=1)

    by_parity = hartley(size_x).reshape(size_x, blocks, 2)
    even_odd = by_parity.transpose(2, 0, 1).reshape(2 * size_x, blocks)
    odd_last = by_parity.transpose(2, 1, 0).reshape(size_x, size_x)
    tables = (
        pieces(planes_table(size_z), 0),
        pieces(planes_table(size_z).T, 0),
        pieces(hartley(size_y), 1),
        pieces(even_odd, 1),
        pieces(odd_last, 1),
    )

    vmem = pl.BlockSpec(memory_space=pltpu.VMEM)
    smem = pl.BlockSpec(memory_space=pltpu.SMEM)
    field = pl.pallas_call(
        functools.partial(exchange_kernel, (blocks, size_x, size_y, size_z)),
        out_shape=jax.ShapeDtypeStruct((nbands, plane_rows, size_z), f32),
        in_specs=[smem, smem] + [vmem] * (1 + len(tables)),
        out_specs=vmem,
        scratch_shapes=[
            pltpu.VMEM((2, 2 * blocks, half_y, size_z), f32),
            pltpu.VMEM((2, blocks, size_y, size_z), f32),
            pltpu.VMEM((2, size_y * blocks, size_z), f32),
            pltpu.VMEM((2, half_y, size_x, size_z), f32),
            pltpu.VMEM((2, 2 * blocks, half_y, size_z), f32),
            pltpu.SemaphoreType.DMA,
            pltpu.SemaphoreType.DMA((2, blocks)),
            pltpu.SemaphoreType.DMA,
            pltpu.SemaphoreType.DMA((2, blocks)),
        ],
        compiler_params=pltpu.CompilerParams(
            collective_id=0, has_side_effects=True, vmem_limit_bytes=60 * MIB
        ),
    )(rows, weights, orbitals.reshape(nbands, plane_rows, size_z), *tables)
    placed = pl.pallas_call(
        functools.partial(place_kernel, nbands),
        out_shape=jax.ShapeDtypeStruct((nbands, plane_rows, size_z), f32),
        in_specs=[smem, vmem],
        out_specs=pl.BlockSpec(memory_space=pl.ANY),
        scratch_shapes=[pltpu.SemaphoreType.DMA((nbands,))],
    )(rows, field)
    return placed.reshape(orbitals.shape)


def solution(mesh):
    return jax.shard_map(
        local,
        mesh=mesh,
        in_specs=(P(None, "blk", "grp", None), P(), P(), P()),
        out_specs=P(None, "blk", "grp", None),
        check_vma=False,
    )
```

```python
import functools
import itertools
import math
import random

import jax
import jax.numpy as jnp
import ml_dtypes
import numpy as np
from jax import lax
from jax.experimental import pallas as pl
from jax.experimental.pallas import tpu as pltpu
from jax.sharding import PartitionSpec as P

screening = 0.05
MESH = pl.DeviceIdType.MESH
MIB = 2**20
f32 = jnp.float32


def hartley(length):
    index = np.arange(length)
    angle = 2.0 * math.pi / length * (index[:, None] * index[None, :] % length)
    return np.cos(angle) + np.sin(angle)


def pieces(table, axis):
    high = table.astype(ml_dtypes.bfloat16)
    low = (table - high.astype(np.float64)).astype(ml_dtypes.bfloat16)
    return jnp.asarray(np.concatenate([high, high, low], axis=axis))


def split(value, axis):
    high = value.astype(jnp.bfloat16)
    low = (value - high.astype(f32)).astype(jnp.bfloat16)
    return jnp.concatenate([high, low, high], axis=axis)


def times_right(value, table):
    return jnp.dot(split(value, 1), table, preferred_element_type=f32)


def times_left(table, value):
    return jnp.dot(table, split(value, 0), preferred_element_type=f32)


def planes_table(size_z):
    half = size_z // 2
    table = hartley(size_z)
    full = np.zeros((2, size_z, 2, 2, half))
    for plane in range(2):
        for part in range(2):
            full[plane, :, part, plane, :] = table[:, part * half : (part + 1) * half]
    return full.reshape(2 * size_z, 2 * size_z)


def torus_of(blocks):
    return (4, 4, 4) if blocks == 64 else (blocks // 2, 1, 2)


def message_order(blocks):
    torus = torus_of(blocks)
    everywhere = itertools.product(*(range(size) for size in torus))
    triples, seen = [], {(0, 0, 0)}
    for offset in everywhere:
        if offset not in seen:
            turns = [offset]
            if torus[0] == torus[1] == torus[2]:
                turns = list(dict.fromkeys(offset[k:] + offset[:k] for k in range(3)))
            seen.update(turns)
            triples.append(turns)
    random.Random(1).shuffle(triples)
    triples.sort(key=lambda turns: sum(min(d, n - d) for d, n in zip(turns[0], torus)))
    mixed = []
    while triples:
        mixed.append(triples.pop(0))
        if triples:
            mixed.append(triples.pop())
    order = [(0, 0, 0, 1)]
    order += [d + (core,) for turns in mixed for core in (0, 1) for d in turns]
    return order + [(0, 0, 0, 0)]


def source_order(blocks, parity):
    torus = torus_of(blocks)
    due = {}
    for time, (dx, dy, dz, core) in enumerate(message_order(blocks)):
        sign = -1 if core else 1
        offset = [sign * d % n for d, n in zip((dx, dy, dz), torus)]
        block = (offset[0], offset[1], (parity - offset[2]) % torus[2] // 2, core)
        due[block] = (time, tuple(offset) + (core,))
    own = (0, 0, parity // 2, 0)
    rest = sorted(due[block] for block in due if block != own)
    return [(0, 0, 0, 0)] + [offset for time, offset in rest]


def packed(order):
    codes = [dx + 4 * dy + 16 * dz + 64 * core for dx, dy, dz, core in order]
    return [sum(c * 128**j for j, c in enumerate(codes[i : i + 4])) for i in range(0, len(codes), 4)]


def word_at(words, index):
    word = jnp.int32(words[0])
    for k in range(1, len(words)):
        word = jnp.where(index == k, jnp.int32(words[k]), word)
    return word


def offsets_in(word):
    for j in range(4):
        code = word // 128**j % 128
        yield code % 4, code // 4 % 4, code // 16 % 4, code // 64


def squared(index, length):
    folded = jnp.where(index <= length // 2, index, index - length).astype(f32)
    return (2.0 * math.pi / length * folded) ** 2


def exchange_kernel(
    sizes,
    rows_ref,
    weight_ref,
    orbitals_ref,
    forward_z_ref,
    inverse_z_ref,
    left_y_ref,
    forward_x_ref,
    inverse_x_ref,
    out_ref,
    phi_ref,
    field_ref,
    outgoing,
    grid,
    turned,
    kernel_table,
    arrived,
    out_sem,
    in_sem,
    back_out_sem,
    back_in_sem,
    load_sem,
):
    blocks, size_x, size_y, size_z = sizes
    half_y = size_y // 2
    half_z = size_z // 2
    blk = lax.axis_index("blk")
    grp = lax.axis_index("grp")
    me = blk * 2 + grp
    own_rows = pl.ds(grp * half_y, half_y)

    span_x, span_y, span_z = torus_of(blocks)
    core = blk % 2
    at_x = blk // 2 % span_x
    at_y = blk // (span_x * span_z)
    at_z = blk // (2 * span_x) % (span_z // 2) * 2 + grp
    sign = 1 - 2 * core
    messages = packed(message_order(blocks))
    sources = [packed(source_order(blocks, parity)) for parity in range(2)]

    def device(offset, direction):
        x, y, z, other_core = offset
        x = (at_x + direction * x + span_x) % span_x
        y = (at_y + direction * y + span_y) % span_y
        z = (at_z + direction * z + span_z) % span_z
        block = (y * (span_z // 2) + z // 2) * span_x + x
        return block * 2 + (core + other_core) % 2, z % 2

    def targets(index):
        return [device(offset, sign) for offset in offsets_in(word_at(messages, index))]

    def source_blocks(index):
        pairs = [word_at(sources[parity], index) for parity in range(2)]
        word = jnp.where((core + grp) % 2 == 0, pairs[0], pairs[1])
        return [device(offset, -sign)[0] for offset in offsets_in(word)]

    count = 2 * blocks

    def every_other(act):
        @pl.loop(0, count // 4 - 1)
        def _(index):
            for j, target in enumerate(targets(index)):
                act(index * 4 + j, target)

        for j, target in enumerate(targets(count // 4 - 1)[:3]):
            act(count - 4 + j, target)

    load = pltpu.make_async_copy(orbitals_ref, phi_ref, load_sem)
    load.start()
    barrier = pltpu.get_barrier_semaphore()

    def greet(slot, target):
        pl.semaphore_signal(barrier, inc=1, device_id=target, device_id_type=MESH)

    every_other(greet)
    pl.semaphore_wait(barrier, count - 1)
    load.wait()

    def density(position, offset):
        first = phi_ref[rows_ref[position]]
        second = phi_ref[rows_ref[(position + blocks - offset) % blocks]]
        value = first * second
        return jnp.concatenate([value[:half_y], value[half_y:]], axis=1)

    def send(part, slot, target):
        pltpu.make_async_remote_copy(
            src_ref=outgoing.at[part, slot],
            dst_ref=grid.at[part, blk, own_rows],
            send_sem=out_sem,
            recv_sem=in_sem.at[part, blk],
            device_id=target,
            device_id_type=MESH,
        ).start()

    def prepare(index, sent):
        at = targets(index)
        value = jnp.concatenate([density(b, side + 1) for b, side in at], axis=0)
        value = times_right(value, forward_z_ref[...])
        for j in range(4):
            for part in range(2):
                outgoing[part, index * 4 + j] = value[
                    j * half_y : (j + 1) * half_y, part * size_z : (part + 1) * size_z
                ]
        for j in range(sent):
            send(0, index * 4 + j, at[j])

    @pl.loop(0, count // 4 - 1)
    def _(index):
        prepare(index, 4)

    prepare(count // 4 - 1, 3)
    every_other(functools.partial(send, 1))
    for part in range(2):
        grid[part, blk, own_rows] = outgoing[part, count - 1]
    field_ref[...] = jnp.zeros_like(field_ref)

    lane = lax.broadcasted_iota(jnp.int32, (size_x, size_z), 1)
    first_half = lane < half_z
    lane_half = jnp.where(first_half, 0, 1)

    def fill_table(part):
        square_x = squared(lax.broadcasted_iota(jnp.int32, (size_x, size_z), 0), size_x)
        square_z = squared(lane - half_z * lane_half + part * half_z, size_z)

        @pl.loop(0, half_y)
        def _(pair):
            total = square_x + squared(2 * pair + lane_half, size_y) + square_z
            safe_total = jnp.where(total > 0, total, 1.0)
            screened = (1.0 - jnp.exp(-safe_total / (4.0 * screening**2))) / safe_total
            value = jnp.where(total > 0, screened, 1.0 / (4.0 * screening**2))
            kernel_table[part, pair] = value * (1.0 / (size_x * size_y * size_z))

    def await_copy(ref, sem):
        pltpu.make_async_copy(ref, ref, sem).wait()

    def turn(part, index, with_own):
        at = source_blocks(index)
        for j, source in enumerate(at):
            if with_own and j == 0:
                await_copy(grid.at[part, blk, own_rows], in_sem.at[part, blk])
            else:
                await_copy(grid.at[part, source], in_sem.at[part, source])
        value = jnp.concatenate([grid[part, source] for source in at], axis=1)
        value = times_left(left_y_ref[...], value)
        for j, source in enumerate(at):
            turned[part, pl.ds(source, size_y, stride=blocks), :] = value[:, j * size_z : (j + 1) * size_z]

    def middle(part):
        group = 4
        mask = first_half[:blocks]

        @pl.loop(0, half_y // group)
        def _(index):
            pairs = [index * group + j for j in range(group)]
            lines = [2 * i + j for i in pairs for j in range(2)]
            value = [turned[part, pl.ds(k * blocks, blocks), :] for k in lines]
            both = times_left(forward_x_ref[...], jnp.concatenate(value, axis=1))
            value = []
            for j in range(group):
                a = both[:, 2 * j * size_z : (2 * j + 1) * size_z]
                b = both[:, (2 * j + 1) * size_z : (2 * j + 2) * size_z]
                stay = jnp.where(first_half, a[:size_x], b[size_x:])
                move = jnp.where(first_half, b[:size_x], a[size_x:])
                value.append((stay + pltpu.roll(move, half_z, 1)) * kernel_table[part, pairs[j]])
            both = times_left(inverse_x_ref[...], jnp.concatenate(value, axis=1))
            for j, i in enumerate(pairs):
                even = both[:blocks, j * size_z : (j + 1) * size_z]
                odd = both[blocks:, j * size_z : (j + 1) * size_z]
                moved = pltpu.roll(jnp.where(mask, odd, even), half_z, 1)
                turned[part, pl.ds(2 * i * blocks, blocks), :] = jnp.where(mask, even, moved)
                turned[part, pl.ds((2 * i + 1) * blocks, blocks), :] = jnp.where(mask, moved, odd)

    def turn_back(part, slot, target):
        block, side = target
        rows = pl.ds(pl.multiple_of(side * half_y, half_y), half_y)
        lines = turned[part, pl.ds(block, size_y, stride=blocks), :]
        grid[part, block, rows] = times_left(left_y_ref[rows, :], lines)

    def send_back(part, slot, target):
        block, side = target
        pltpu.make_async_remote_copy(
            src_ref=grid.at[part, block, pl.ds(side * half_y, half_y)],
            dst_ref=arrived.at[part, me],
            send_sem=back_out_sem,
            recv_sem=back_in_sem.at[part, blk],
            device_id=target,
            device_id_type=MESH,
        ).start()

    def turn_all(part):
        fill_table(part)
        turn(part, 0, True)

        @pl.loop(1, blocks // 4)
        def _(index):
            turn(part, index, False)

    def give_back(part, index, sent):
        at = targets(index)
        for target in at:
            turn_back(part, None, target)
        for target in at[:sent]:
            send_back(part, None, target)

    turn_all(0)
    middle(0)

    @pl.loop(0, count // 4)
    def _(index):
        for target in targets(index):
            turn_back(0, None, target)

    turn_all(1)
    every_other(functools.partial(send_back, 0))
    middle(1)

    @pl.loop(0, count // 4 - 1)
    def _(index):
        give_back(1, index, 4)

    give_back(1, count // 4 - 1, 3)
    for part in range(2):
        arrived[part, me] = grid[part, blk, own_rows]

    def collect(index, with_own):
        at = source_blocks(index)
        for part in range(2):
            for j, source in enumerate(at):
                if with_own and j == 0:
                    await_copy(arrived.at[part, me], back_in_sem.at[part, blk])
                else:
                    landed = arrived.at[part, pl.ds(source * 2, 2)]
                    await_copy(landed, back_in_sem.at[part, source])
        slots = [source * 2 + side for source in at for side in range(2)]
        value = [jnp.concatenate([arrived[0, k], arrived[1, k]], axis=1) for k in slots]
        value = times_right(jnp.concatenate(value, axis=0), inverse_z_ref[...])
        for j, position in enumerate(at):
            own = weight_ref[rows_ref[position]] * phi_ref[rows_ref[position]]
            total = jnp.zeros((size_y, size_z), f32)
            for side in range(2):
                behind = (position + blocks - side - 1) % blocks
                term = value[(2 * j + side) * half_y : (2 * j + side + 1) * half_y]
                term = jnp.concatenate([term[:, :size_z], term[:, size_z:]], axis=0)
                total = total + term * (weight_ref[rows_ref[behind]] * phi_ref[rows_ref[behind]])
                field_ref[behind] += term * own
            field_ref[position] += total

    collect(0, True)

    @pl.loop(1, blocks // 4)
    def _(index):
        collect(index, False)

    @pl.loop(0, blocks)
    def _(band):
        out_ref[band] = field_ref[rows_ref[blocks + band]]

    for part in range(2):
        sent = outgoing.at[part, pl.ds(0, count - 1)]
        await_copy(sent, out_sem)
        await_copy(sent, back_out_sem)


def local(orbitals, occupations, band_block, cycle):
    blocks = lax.axis_size("blk")
    nbands, local_x, half_y, size_z = orbitals.shape
    size_x = local_x * blocks
    size_y = half_y * 2
    plane_rows = local_x * half_y

    names = jnp.concatenate([cycle, band_block])
    listed = jnp.concatenate(
        [jnp.broadcast_to(v[None], (nbands, nbands)) for v in (band_block, cycle)]
    )
    index = jnp.arange(nbands, dtype=jnp.int32)[None]
    rows = jnp.sum(jnp.where(names[:, None] == listed, index, 0), axis=1)

    by_parity = hartley(size_x).reshape(size_x, blocks, 2)
    even_odd = by_parity.transpose(2, 0, 1).reshape(2 * size_x, blocks)
    odd_last = by_parity.transpose(2, 1, 0).reshape(size_x, size_x)
    tables = (
        pieces(planes_table(size_z), 0),
        pieces(planes_table(size_z).T, 0),
        pieces(hartley(size_y), 1),
        pieces(even_odd, 1),
        pieces(odd_last, 1),
    )

    vmem = pl.BlockSpec(memory_space=pltpu.VMEM)
    smem = pl.BlockSpec(memory_space=pltpu.SMEM)
    field = pl.pallas_call(
        functools.partial(exchange_kernel, (blocks, size_x, size_y, size_z)),
        out_shape=pltpu.VMEM((nbands, plane_rows, size_z), f32),
        in_specs=[smem, smem, pl.BlockSpec(memory_space=pl.ANY)] + [vmem] * len(tables),
        out_specs=vmem,
        scratch_shapes=[
            pltpu.VMEM((nbands, plane_rows, size_z), f32),
            pltpu.VMEM((nbands, plane_rows, size_z), f32),
            pltpu.VMEM((2, 2 * blocks, half_y, size_z), f32),
            pltpu.VMEM((2, blocks, size_y, size_z), f32),
            pltpu.VMEM((2, size_y * blocks, size_z), f32),
            pltpu.VMEM((2, half_y, size_x, size_z), f32),
            pltpu.VMEM((2, 2 * blocks, half_y, size_z), f32),
            pltpu.SemaphoreType.DMA,
            pltpu.SemaphoreType.DMA((2, blocks)),
            pltpu.SemaphoreType.DMA,
            pltpu.SemaphoreType.DMA((2, blocks)),
            pltpu.SemaphoreType.DMA,
        ],
        compiler_params=pltpu.CompilerParams(
            collective_id=0, has_side_effects=True, vmem_limit_bytes=55 * MIB
        ),
    )(rows, occupations, orbitals.reshape(nbands, plane_rows, size_z), *tables)
    return field.reshape(orbitals.shape)


def solution(mesh):
    return jax.shard_map(
        local,
        mesh=mesh,
        in_specs=(P(None, "blk", "grp", None), P(), P(), P()),
        out_specs=P(None, "blk", "grp", None),
        check_vma=False,
    )
```

```python
import functools
import itertools
import math
import random

import jax
import jax.numpy as jnp
import ml_dtypes
import numpy as np
from jax import lax
from jax.experimental import pallas as pl
from jax.experimental.pallas import tpu as pltpu
from jax.sharding import PartitionSpec as P

screening = 0.05
MESH = pl.DeviceIdType.MESH
MIB = 2**20
f32 = jnp.float32


def hartley(length):
    index = np.arange(length)
    angle = 2.0 * math.pi / length * (index[:, None] * index[None, :] % length)
    return np.cos(angle) + np.sin(angle)


def pieces(table, axis):
    high = table.astype(ml_dtypes.bfloat16)
    low = (table - high.astype(np.float64)).astype(ml_dtypes.bfloat16)
    return jnp.asarray(np.concatenate([high, high, low], axis=axis))


def split(value, axis):
    high = value.astype(jnp.bfloat16)
    low = (value - high.astype(f32)).astype(jnp.bfloat16)
    return jnp.concatenate([high, low, high], axis=axis)


def times_right(value, table):
    return jnp.dot(split(value, 1), table, preferred_element_type=f32)


def times_left(table, value):
    return jnp.dot(table, split(value, 0), preferred_element_type=f32)


def planes_table(size_z):
    half = size_z // 2
    table = hartley(size_z)
    full = np.zeros((2, size_z, 2, 2, half))
    for plane in range(2):
        for part in range(2):
            full[plane, :, part, plane, :] = table[:, part * half : (part + 1) * half]
    return full.reshape(2 * size_z, 2 * size_z)


def torus_of(blocks):
    return (4, 4, 4) if blocks == 64 else (blocks // 2, 1, 2)


def message_order(blocks):
    torus = torus_of(blocks)
    everywhere = itertools.product(*(range(size) for size in torus))
    triples, seen = [], {(0, 0, 0)}
    for offset in everywhere:
        if offset not in seen:
            turns = [offset]
            if torus[0] == torus[1] == torus[2]:
                turns = list(dict.fromkeys(offset[k:] + offset[:k] for k in range(3)))
            seen.update(turns)
            triples.append(turns)
    random.Random(1).shuffle(triples)
    triples.sort(key=lambda turns: sum(min(d, n - d) for d, n in zip(turns[0], torus)))
    mixed = []
    while triples:
        mixed.append(triples.pop(0))
        if triples:
            mixed.append(triples.pop())
    order = [(0, 0, 0, 1)]
    order += [d + (core,) for turns in mixed for core in (0, 1) for d in turns]
    return order + [(0, 0, 0, 0)]


def source_order(blocks, parity):
    torus = torus_of(blocks)
    due = {}
    for time, (dx, dy, dz, core) in enumerate(message_order(blocks)):
        sign = -1 if core else 1
        offset = [sign * d % n for d, n in zip((dx, dy, dz), torus)]
        block = (offset[0], offset[1], (parity - offset[2]) % torus[2] // 2, core)
        due[block] = (time, tuple(offset) + (core,))
    own = (0, 0, parity // 2, 0)
    rest = sorted(due[block] for block in due if block != own)
    return [(0, 0, 0, 0)] + [offset for time, offset in rest]


def packed(order):
    codes = [dx + 4 * dy + 16 * dz + 64 * core for dx, dy, dz, core in order]
    return [sum(c * 128**j for j, c in enumerate(codes[i : i + 4])) for i in range(0, len(codes), 4)]


def word_at(words, index):
    word = jnp.int32(words[0])
    for k in range(1, len(words)):
        word = jnp.where(index == k, jnp.int32(words[k]), word)
    return word


def offsets_in(word):
    for j in range(4):
        code = word // 128**j % 128
        yield code % 4, code // 4 % 4, code // 16 % 4, code // 64


def squared(index, length):
    folded = jnp.where(index <= length // 2, index, index - length).astype(f32)
    return (2.0 * math.pi / length * folded) ** 2


def exchange_kernel(
    sizes,
    weight_ref,
    band_block_ref,
    cycle_ref,
    orbitals_ref,
    forward_z_ref,
    inverse_z_ref,
    left_y_ref,
    forward_x_ref,
    inverse_x_ref,
    out_ref,
    phi_ref,
    field_ref,
    outgoing,
    grid,
    turned,
    kernel_table,
    arrived,
    out_sem,
    in_sem,
    back_out_sem,
    back_in_sem,
    load_sem,
    listing,
    listed,
    list_sem,
):
    blocks, size_x, size_y, size_z = sizes
    half_y = size_y // 2
    half_z = size_z // 2
    blk = lax.axis_index("blk")
    grp = lax.axis_index("grp")
    me = blk * 2 + grp
    own_rows = pl.ds(grp * half_y, half_y)

    span_x, span_y, span_z = torus_of(blocks)
    core = blk % 2
    at_x = blk // 2 % span_x
    at_y = blk // (span_x * span_z)
    at_z = blk // (2 * span_x) % (span_z // 2) * 2 + grp
    sign = 1 - 2 * core
    messages = packed(message_order(blocks))
    sources = [packed(source_order(blocks, parity)) for parity in range(2)]

    def device(offset, direction):
        x, y, z, other_core = offset
        x = (at_x + direction * x + span_x) % span_x
        y = (at_y + direction * y + span_y) % span_y
        z = (at_z + direction * z + span_z) % span_z
        block = (y * (span_z // 2) + z // 2) * span_x + x
        return block * 2 + (core + other_core) % 2, z % 2

    def targets(index):
        return [device(offset, sign) for offset in offsets_in(word_at(messages, index))]

    def source_blocks(index):
        pairs = [word_at(sources[parity], index) for parity in range(2)]
        word = jnp.where((core + grp) % 2 == 0, pairs[0], pairs[1])
        return [device(offset, -sign)[0] for offset in offsets_in(word)]

    count = 2 * blocks

    def every_other(act):
        @pl.loop(0, count // 4 - 1)
        def _(index):
            for j, target in enumerate(targets(index)):
                act(index * 4 + j, target)

        for j, target in enumerate(targets(count // 4 - 1)[:3]):
            act(count - 4 + j, target)

    load = pltpu.make_async_copy(orbitals_ref, phi_ref, load_sem)
    load.start()

    listing[...] = jnp.zeros_like(listing)
    for row, (named, among) in enumerate(((cycle_ref, band_block_ref), (band_block_ref, cycle_ref))):
        named = jnp.broadcast_to(named[...], (blocks, blocks))
        among = jnp.broadcast_to(among[...], (blocks, blocks)).T
        index = lax.broadcasted_iota(jnp.int32, (blocks, blocks), 0)
        found = jnp.max(jnp.where(named == among, index, 0), axis=0, keepdims=True)
        listing[row : row + 1, :blocks] = found
    to_scalars = pltpu.make_async_copy(listing, listed, list_sem)
    to_scalars.start()

    barrier = pltpu.get_barrier_semaphore()

    def greet(slot, target):
        pl.semaphore_signal(barrier, inc=1, device_id=target, device_id_type=MESH)

    every_other(greet)
    pl.semaphore_wait(barrier, count - 1)
    load.wait()
    to_scalars.wait()

    def density(position, offset):
        first = phi_ref[listed[0, position]]
        second = phi_ref[listed[0, (position + blocks - offset) % blocks]]
        value = first * second
        return jnp.concatenate([value[:half_y], value[half_y:]], axis=1)

    def send(part, slot, target):
        pltpu.make_async_remote_copy(
            src_ref=outgoing.at[part, slot],
            dst_ref=grid.at[part, blk, own_rows],
            send_sem=out_sem,
            recv_sem=in_sem.at[part, blk],
            device_id=target,
            device_id_type=MESH,
        ).start()

    def prepare(index, sent):
        at = targets(index)
        value = jnp.concatenate([density(b, side + 1) for b, side in at], axis=0)
        value = times_right(value, forward_z_ref[...])
        for j in range(4):
            for part in range(2):
                outgoing[part, index * 4 + j] = value[
                    j * half_y : (j + 1) * half_y, part * size_z : (part + 1) * size_z
                ]
        for j in range(sent):
            send(0, index * 4 + j, at[j])

    @pl.loop(0, count // 4 - 1)
    def _(index):
        prepare(index, 4)

    prepare(count // 4 - 1, 3)
    every_other(functools.partial(send, 1))
    for part in range(2):
        grid[part, blk, own_rows] = outgoing[part, count - 1]
    field_ref[...] = jnp.zeros_like(field_ref)

    lane = lax.broadcasted_iota(jnp.int32, (size_x, size_z), 1)
    first_half = lane < half_z
    lane_half = jnp.where(first_half, 0, 1)

    def fill_table(part):
        square_x = squared(lax.broadcasted_iota(jnp.int32, (size_x, size_z), 0), size_x)
        square_z = squared(lane - half_z * lane_half + part * half_z, size_z)

        @pl.loop(0, half_y)
        def _(pair):
            total = square_x + squared(2 * pair + lane_half, size_y) + square_z
            safe_total = jnp.where(total > 0, total, 1.0)
            screened = (1.0 - jnp.exp(-safe_total / (4.0 * screening**2))) / safe_total
            value = jnp.where(total > 0, screened, 1.0 / (4.0 * screening**2))
            kernel_table[part, pair] = value * (1.0 / (size_x * size_y * size_z))

    def await_copy(ref, sem):
        pltpu.make_async_copy(ref, ref, sem).wait()

    def turn(part, index, with_own, between=None):
        at = source_blocks(index)
        for j, source in enumerate(at):
            if with_own and j == 0:
                await_copy(grid.at[part, blk, own_rows], in_sem.at[part, blk])
            else:
                await_copy(grid.at[part, source], in_sem.at[part, source])
        if between is not None:
            between()
        value = jnp.concatenate([grid[part, source] for source in at], axis=1)
        value = times_left(left_y_ref[...], value)
        for j, source in enumerate(at):
            turned[part, pl.ds(source, size_y, stride=blocks), :] = value[:, j * size_z : (j + 1) * size_z]

    def middle(part):
        group = 4
        mask = first_half[:blocks]

        @pl.loop(0, half_y // group)
        def _(index):
            pairs = [index * group + j for j in range(group)]
            lines = [2 * i + j for i in pairs for j in range(2)]
            value = [turned[part, pl.ds(k * blocks, blocks), :] for k in lines]
            both = times_left(forward_x_ref[...], jnp.concatenate(value, axis=1))
            value = []
            for j in range(group):
                a = both[:, 2 * j * size_z : (2 * j + 1) * size_z]
                b = both[:, (2 * j + 1) * size_z : (2 * j + 2) * size_z]
                stay = jnp.where(first_half, a[:size_x], b[size_x:])
                move = jnp.where(first_half, b[:size_x], a[size_x:])
                value.append((stay + pltpu.roll(move, half_z, 1)) * kernel_table[part, pairs[j]])
            both = times_left(inverse_x_ref[...], jnp.concatenate(value, axis=1))
            for j, i in enumerate(pairs):
                even = both[:blocks, j * size_z : (j + 1) * size_z]
                odd = both[blocks:, j * size_z : (j + 1) * size_z]
                moved = pltpu.roll(jnp.where(mask, odd, even), half_z, 1)
                turned[part, pl.ds(2 * i * blocks, blocks), :] = jnp.where(mask, even, moved)
                turned[part, pl.ds((2 * i + 1) * blocks, blocks), :] = jnp.where(mask, moved, odd)

    def turn_back(part, slot, target):
        block, side = target
        rows = pl.ds(pl.multiple_of(side * half_y, half_y), half_y)
        lines = turned[part, pl.ds(block, size_y, stride=blocks), :]
        grid[part, block, rows] = times_left(left_y_ref[rows, :], lines)

    def send_back(part, slot, target):
        block, side = target
        pltpu.make_async_remote_copy(
            src_ref=grid.at[part, block, pl.ds(side * half_y, half_y)],
            dst_ref=arrived.at[part, me],
            send_sem=back_out_sem,
            recv_sem=back_in_sem.at[part, blk],
            device_id=target,
            device_id_type=MESH,
        ).start()

    def turn_all(part, then=None):
        fill_table(part)
        turn(part, 0, True)

        @pl.loop(1, blocks // 4 - 1)
        def _(index):
            turn(part, index, False)

        turn(part, blocks // 4 - 1, False, then)

    def give_back(part, index, sent):
        at = targets(index)
        for target in at:
            turn_back(part, None, target)
        for target in at[:sent]:
            send_back(part, None, target)

    turn_all(0)
    middle(0)

    @pl.loop(0, count // 4)
    def _(index):
        for target in targets(index):
            turn_back(0, None, target)

    def start_return():
        every_other(functools.partial(send_back, 0))

    turn_all(1, start_return)
    middle(1)

    @pl.loop(0, count // 4 - 1)
    def _(index):
        give_back(1, index, 4)

    give_back(1, count // 4 - 1, 3)
    for part in range(2):
        arrived[part, me] = grid[part, blk, own_rows]

    def collect(index, with_own):
        at = source_blocks(index)
        for part in range(2):
            for j, source in enumerate(at):
                if with_own and j == 0:
                    await_copy(arrived.at[part, me], back_in_sem.at[part, blk])
                else:
                    landed = arrived.at[part, pl.ds(source * 2, 2)]
                    await_copy(landed, back_in_sem.at[part, source])
        slots = [source * 2 + side for source in at for side in range(2)]
        value = [jnp.concatenate([arrived[0, k], arrived[1, k]], axis=1) for k in slots]
        value = times_right(jnp.concatenate(value, axis=0), inverse_z_ref[...])
        for j, position in enumerate(at):
            own = weight_ref[listed[0, position]] * phi_ref[listed[0, position]]
            total = jnp.zeros((size_y, size_z), f32)
            for side in range(2):
                behind = (position + blocks - side - 1) % blocks
                term = value[(2 * j + side) * half_y : (2 * j + side + 1) * half_y]
                term = jnp.concatenate([term[:, :size_z], term[:, size_z:]], axis=0)
                total = total + term * (weight_ref[listed[0, behind]] * phi_ref[listed[0, behind]])
                field_ref[behind] += term * own
            field_ref[position] += total

    collect(0, True)

    @pl.loop(1, blocks // 4)
    def _(index):
        collect(index, False)

    @pl.loop(0, blocks)
    def _(band):
        out_ref[band] = field_ref[listed[1, band]]

    for part in range(2):
        sent = outgoing.at[part, pl.ds(0, count - 1)]
        await_copy(sent, out_sem)
        await_copy(sent, back_out_sem)


def local(orbitals, occupations, band_block, cycle):
    blocks = lax.axis_size("blk")
    nbands, local_x, half_y, size_z = orbitals.shape
    size_x = local_x * blocks
    size_y = half_y * 2
    plane_rows = local_x * half_y

    by_parity = hartley(size_x).reshape(size_x, blocks, 2)
    even_odd = by_parity.transpose(2, 0, 1).reshape(2 * size_x, blocks)
    odd_last = by_parity.transpose(2, 1, 0).reshape(size_x, size_x)
    tables = (
        pieces(planes_table(size_z), 0),
        pieces(planes_table(size_z).T, 0),
        pieces(hartley(size_y), 1),
        pieces(even_odd, 1),
        pieces(odd_last, 1),
    )

    vmem = pl.BlockSpec(memory_space=pltpu.VMEM)
    smem = pl.BlockSpec(memory_space=pltpu.SMEM)
    field = pl.pallas_call(
        functools.partial(exchange_kernel, (blocks, size_x, size_y, size_z)),
        out_shape=pltpu.VMEM((nbands, plane_rows, size_z), f32),
        in_specs=[smem, vmem, vmem, pl.BlockSpec(memory_space=pl.ANY)] + [vmem] * len(tables),
        out_specs=vmem,
        scratch_shapes=[
            pltpu.VMEM((nbands, plane_rows, size_z), f32),
            pltpu.VMEM((nbands, plane_rows, size_z), f32),
            pltpu.VMEM((2, 2 * blocks, half_y, size_z), f32),
            pltpu.VMEM((2, blocks, size_y, size_z), f32),
            pltpu.VMEM((2, size_y * blocks, size_z), f32),
            pltpu.VMEM((2, half_y, size_x, size_z), f32),
            pltpu.VMEM((2, 2 * blocks, half_y, size_z), f32),
            pltpu.SemaphoreType.DMA,
            pltpu.SemaphoreType.DMA((2, blocks)),
            pltpu.SemaphoreType.DMA,
            pltpu.SemaphoreType.DMA((2, blocks)),
            pltpu.SemaphoreType.DMA,
            pltpu.VMEM((8, 128), jnp.int32),
            pltpu.SMEM((8, 128), jnp.int32),
            pltpu.SemaphoreType.DMA,
        ],
        compiler_params=pltpu.CompilerParams(
            collective_id=0, has_side_effects=True, vmem_limit_bytes=55 * MIB
        ),
    )(
        occupations,
        band_block.reshape(1, nbands),
        cycle.reshape(1, nbands),
        orbitals.reshape(nbands, plane_rows, size_z),
        *tables,
    )
    return field.reshape(orbitals.shape)


def solution(mesh):
    return jax.shard_map(
        local,
        mesh=mesh,
        in_specs=(P(None, "blk", "grp", None), P(), P(), P()),
        out_specs=P(None, "blk", "grp", None),
        check_vma=False,
    )
```
